32 devices in a mesh: groups: 2 (over x), ctx: 16 (over z, y, core).
Axes of the slice: x: 2, y: 2, z: 4, core: 2. Of those that a mesh axis runs over, the one named last changes fastest.
Arguments:
- queries: bfloat16 [64, 8192], P(('groups', 'ctx')), parts along dimension 0, may hold values from -256 to 256, as said below
- cached_key_rows: bfloat16 [16384, 1024], P(('groups', 'ctx')), parts along dimension 0, may hold values from -4 to 4, as said below
- cached_value_rows: bfloat16 [16384, 1024], P(('groups', 'ctx')), parts along dimension 0, may hold values from -6 to 6
- cache_position: int32 [16384], P(('groups', 'ctx')), parts along dimension 0, may hold values from 0 to 8191, as said below
- lengths: int32 [64], P(('groups', 'ctx')), parts along dimension 0, may hold values from 2 to 8192, as said below
- norm_gain: float32 [8192], replicated, may hold values from 0.5 to 1.5
- gate_weight: bfloat16 [14336, 8192], P('ctx'), may hold values from -0.0625 to 0.0625
- up_weight: bfloat16 [14336, 8192], P('ctx'), may hold values from -0.0625 to 0.0625
- down_weight: bfloat16 [14336, 8192], P('ctx'), may hold values from -0.046875 to 0.046875
Outputs:
- layer_out: bfloat16 [64, 8192], P(('groups', 'ctx')), parts along dimension 0
The draws below stay inside these ranges and needn't reach their ends.
There are 2 independent parts, one for each index of `groups`. The reference program is written for one: setup_inputs(seed, part) draws one part's arguments, and reference() takes and returns one part's arrays. A program takes and returns all parts, laid end to end along the dimension named above; an argument that names none is the same for every part. Nothing has to cross between parts.
Inputs may be any that keep to these rules, and one draw needn't show every extreme that they name: `queries`: queries stay within the stated range. `cached_key_rows`: keys stay within the stated range. `cache_position`: A permutation of 0 to 8191. `lengths`: some row has length 8192 and some row has length 2.
All inputs are finite; a program needn't handle non-finite values.
Results may differ from the reference program's by a relative error of at most 0.02.
Values may be sent and summed in bfloat16 or wider, within the bound.
A program may use at most 128 MiB of HBM per device.

```python
import jax
import jax.numpy as jnp
from jax import lax

D = 8192
QUERY_HEADS = 64
KEY_VALUE_HEADS = 8
HEAD_SIZE = 128
FFH = 14336
ROWS = 32
CACHE_SLOTS = 8192


def cache_order(key):
    return jax.random.permutation(jax.random.fold_in(key, 11), CACHE_SLOTS).astype(jnp.int32)


def random_base_keys(key):
    sampled_entries = jax.random.normal(jax.random.fold_in(key, 23), (CACHE_SLOTS, KEY_VALUE_HEADS * HEAD_SIZE), jnp.float32)
    return jnp.clip(sampled_entries, -4.0, 4.0)


def draw_cache_position(key, part):
    return cache_order(key)


def draw_cached_key_rows(key, part):
    keyed = random_base_keys(key)
    return keyed.astype(jnp.bfloat16)


def draw_queries(key, part):
    sampled_entries = jax.random.normal(jax.random.fold_in(key, 31), (ROWS, QUERY_HEADS * HEAD_SIZE), jnp.float32)
    sampled_entries = jnp.clip(sampled_entries, -4.0, 4.0)
    return sampled_entries.astype(jnp.bfloat16)


def draw_lengths(key, part):
    sampled_entries = jax.random.randint(jax.random.fold_in(key, 53), (ROWS,), 2, CACHE_SLOTS + 1).astype(jnp.int32)
    first_row = jax.random.randint(jax.random.fold_in(key, 59), (), 0, ROWS).astype(jnp.int32)
    offset_row = jax.random.randint(jax.random.fold_in(key, 61), (), 0, ROWS - 1).astype(jnp.int32)
    second_row = (first_row + 1 + offset_row) % ROWS
    sampled_entries = sampled_entries.at[first_row].set(CACHE_SLOTS)
    sampled_entries = sampled_entries.at[second_row].set(2)
    return sampled_entries


def level_of(rng, extent, split, low, high):
    gain, own = 1.0, jax.random.fold_in(rng, 6)
    for position, parts in split:
        steps = jnp.exp(jax.random.uniform(jax.random.fold_in(own, position), (parts,), jnp.float32, low / len(split), high / len(split)))
        gain = gain * jnp.repeat(steps, extent[position] // parts).reshape([-1 if axis == position else 1 for axis in range(len(extent))])
    return gain


def scatter_about(rng, shape, scale, bound, cuts=(), held_as=jnp.bfloat16):
    values = jax.random.normal(rng, shape, jnp.float32) * scale
    if len(cuts) > 0:
        values = level_of(rng, shape, cuts, -0.22, 0.18) * values
    return jnp.clip(values, min=-bound, max=bound).astype(held_as)


def setup_inputs(seed: int = 0, part: int = 0) -> dict:
    key_of = jax.random.split(jax.random.key(seed), 10)
    part_keys = jax.random.split(jax.random.fold_in(key_of[9], part), 10)
    queries = draw_queries(jax.random.fold_in(jax.random.fold_in(key_of[9], part), 71), part)
    cached_key_rows = draw_cached_key_rows(jax.random.fold_in(jax.random.fold_in(key_of[9], part), 71), part)
    cached_value_rows = scatter_about(part_keys[2], (CACHE_SLOTS, KEY_VALUE_HEADS * HEAD_SIZE), 1.0, 6.0, ((0, 16),))
    cache_position = draw_cache_position(jax.random.fold_in(jax.random.fold_in(key_of[9], part), 71), part)
    lengths = draw_lengths(jax.random.fold_in(jax.random.fold_in(key_of[9], part), 71), part)
    norm_gain = jnp.clip(jax.random.uniform(key_of[5], (D,), jnp.float32, 0.5, 1.5), 0.5, 1.5)
    gate_weight = scatter_about(key_of[6], (FFH, D), D ** -0.5, 0.0625, ((0, 16),))
    up_weight = scatter_about(key_of[7], (FFH, D), D ** -0.5, 0.0625, ((0, 16),))
    down_weight = scatter_about(key_of[8], (FFH, D), FFH ** -0.5, 0.046875, ((0, 16),))
    return {"queries": queries, "cached_key_rows": cached_key_rows, "cached_value_rows": cached_value_rows, "cache_position": cache_position, "lengths": lengths, "norm_gain": norm_gain, "gate_weight": gate_weight, "up_weight": up_weight, "down_weight": down_weight}


def reference(queries, cached_key_rows, cached_value_rows, cache_position, lengths, norm_gain, gate_weight, up_weight, down_weight):
    query_group_size = QUERY_HEADS // KEY_VALUE_HEADS
    key_head_count = cached_key_rows.astype(jnp.float32).reshape(CACHE_SLOTS, KEY_VALUE_HEADS, HEAD_SIZE)
    value_head_count = cached_value_rows.astype(jnp.float32).reshape(CACHE_SLOTS, KEY_VALUE_HEADS, HEAD_SIZE)
    count_of_blocks = ROWS // 8
    query_block_list = queries.astype(jnp.float32).reshape(count_of_blocks, 8, KEY_VALUE_HEADS, query_group_size, HEAD_SIZE)
    length_blocks = lengths.reshape(count_of_blocks, 8)

    def attend(pieces):
        query_block, length_block = pieces
        scores = jnp.einsum('rkgd,tkd->rkgt', query_block, key_head_count) * HEAD_SIZE ** (-0.5)
        live = (cache_position[None, :] < length_block[:, None])[:, None, None, :]
        scores = jnp.where(live, scores, -1e+30)
        peak = lax.optimization_barrier(jnp.max(scores, axis=3, keepdims=True))
        weights = jnp.where(live, jnp.exp(scores - peak), 0.0)
        totals = lax.optimization_barrier(jnp.sum(weights, axis=3))
        rounded = lax.optimization_barrier(weights.astype(jnp.bfloat16)).astype(jnp.float32)
        summed = jnp.einsum('rkgt,tkd->rkgd', rounded, value_head_count)
        return (summed / totals[..., None]).reshape(8, D)
    attended = lax.map(attend, (query_block_list, length_blocks)).reshape(ROWS, D).astype(jnp.bfloat16)
    widened = attended.astype(jnp.float32)
    mean_square = lax.optimization_barrier(jnp.mean(widened * widened, axis=1, keepdims=True)) + 1e-05
    normed = (widened * lax.rsqrt(mean_square) * norm_gain[None, :]).astype(jnp.bfloat16)
    gate = jnp.dot(normed, gate_weight.T, preferred_element_type=jnp.float32)
    upward = jnp.dot(normed, up_weight.T, preferred_element_type=jnp.float32)
    activated = (jax.nn.silu(gate) * upward).astype(jnp.bfloat16)
    return jnp.dot(activated, down_weight, preferred_element_type=jnp.float32).astype(jnp.bfloat16)
```

```python
import functools

import jax
import jax.numpy as jnp
from jax import lax
from jax.experimental import pallas as pl
from jax.experimental.pallas import tpu as pltpu
from jax.sharding import PartitionSpec as P

KEY_VALUE_HEADS = 8
GROUP = 8
HEAD_SIZE = 128
EPS = 1e-5
PIECES = 4
MESH = pl.DeviceIdType.MESH
bf16, f32 = jnp.bfloat16, jnp.float32


def columns_of(a, first=0):
    return jnp.stack(
        [
            jnp.broadcast_to(a[:, first + g : first + g + 1], (a.shape[0], HEAD_SIZE))
            for g in range(KEY_VALUE_HEADS)
        ]
    )


def kernel(
    n, rows, q_ref, pos_ref, gain_ref, k_hbm, v_hbm, wg_hbm, wu_hbm, wd_hbm, out_ref,
    k_v, v_v, wg, wu, wd, gathq, gathx, part, stats, xs, act,
    pair_send, pair_recv, pst_send, pst_recv, chip_send, chip_recv, cst_send, cst_recv,
    pair2_send, pair2_recv, chip2_send, chip2_recv,
    load_sem, w_sem, ag_send, ag_fwd, ag_recv, pr_send, pr_recv, ch_send, ch_recv,
):
    me = lax.axis_index("ctx")
    half = n // 2
    core = lax.rem(me, 2)
    chip = me // 2
    partner = me + 1 - 2 * core
    chunk = rows * GROUP
    total_rows = n * chunk
    hidden = wg.shape[0]

    k_copy = pltpu.make_async_copy(k_hbm, k_v, load_sem.at[0])
    v_copy = pltpu.make_async_copy(v_hbm, v_v, load_sem.at[1])
    k_copy.start()
    v_copy.start()
    w_copies = []
    step = hidden // PIECES // 16 * 16
    for i, (src, dst) in enumerate(((wg_hbm, wg), (wu_hbm, wu), (wd_hbm, wd))):
        for j in range(PIECES):
            size = step if j < PIECES - 1 else hidden - step * (PIECES - 1)
            span = pl.ds(j * step, size)
            w_copies.append(
                pltpu.make_async_copy(src.at[span], dst.at[span], w_sem.at[i, j])
            )

    def remote(src, dst, send, recv, to):
        return pltpu.make_async_remote_copy(
            src_ref=src, dst_ref=dst, send_sem=send, recv_sem=recv,
            device_id={"ctx": to}, device_id_type=MESH,
        )

    def loop(lo, hi, body):
        def step(i, carry):
            body(i)
            return carry

        lax.fori_loop(lo, hi, step, 0)

    barrier = pltpu.get_barrier_semaphore()
    pl.semaphore_signal(barrier, inc=1, device_id={"ctx": partner}, device_id_type=MESH)

    def greet(k):
        to = 2 * lax.rem(chip + k, half) + core
        pl.semaphore_signal(barrier, inc=1, device_id={"ctx": to}, device_id_type=MESH)

    loop(1, half, greet)
    gathq[me] = q_ref[...]
    pl.semaphore_wait(barrier, half)

    def gather(buf, which, during=None):
        def copy_to(source, to, send):
            return remote(buf.at[source], buf.at[source], send, ag_recv.at[which, source], to)

        def send(k):
            copy_to(me, 2 * lax.rem(chip + k, half) + core, ag_send.at[which, k]).start()

        copy_to(me, partner, ag_send.at[which, 0]).start()
        loop(1, half, send)
        if during is not None:
            during()

        def forward(k):
            source = 2 * lax.rem(chip + half - k, half) + core
            copy_to(source, partner, ag_fwd.at[which, k]).wait_recv()
            copy_to(source, partner, ag_fwd.at[which, k]).start()

        loop(1, half, forward)

        def arrive(p):
            copy_to(2 * p + 1 - core, partner, ag_send.at[which, 0]).wait_recv()

        loop(0, half, arrive)

        def sent(k):
            copy_to(me, partner, ag_send.at[which, k]).wait_send()

        loop(0, half, sent)

        def forwarded(k):
            source = 2 * lax.rem(chip + half - k, half) + core
            copy_to(source, partner, ag_fwd.at[which, k]).wait_send()

        loop(1, half, forwarded)

    def start_weights():
        for copy in w_copies:
            copy.start()

    gather(gathq, 0, start_weights)

    k_copy.wait()
    v_copy.wait()
    limits = gathq[:, KEY_VALUE_HEADS].reshape(total_rows, HEAD_SIZE).astype(f32)
    limit = limits[:, 0:1] * 256.0 + limits[:, 64:65]
    live = pos_ref[...].astype(f32) < limit
    lane = lax.broadcasted_iota(jnp.int32, (total_rows, HEAD_SIZE), 1)
    stats[...] = jnp.zeros_like(stats)

    def head(g):
        span = pl.ds(pl.multiple_of(g * HEAD_SIZE, HEAD_SIZE), HEAD_SIZE)
        q = gathq[:, g].reshape(total_rows, HEAD_SIZE)
        s = lax.dot_general(
            q, k_v[:, span], (((1,), (1,)), ((), ())), preferred_element_type=f32
        ) * HEAD_SIZE ** (-0.5)
        s = jnp.where(live, s, -1e30)
        m = jnp.max(s, axis=1, keepdims=True)
        w = jnp.where(live, jnp.exp(s - m), 0.0)
        t = jnp.sum(w, axis=1, keepdims=True)
        part[g] = jnp.dot(w.astype(bf16), v_v[:, span], preferred_element_type=f32)
        stats[...] = jnp.where(lane == g, m, jnp.where(lane == 64 + g, t, stats[...]))

    loop(0, KEY_VALUE_HEADS, head)

    small = lax.broadcasted_iota(jnp.int32, (chunk, HEAD_SIZE), 1)

    def slab(d):
        return pl.ds(pl.multiple_of(d * chunk, chunk), chunk)

    def pair_copy(which, p):
        src, dst = ((pair_send, pair_recv), (pst_send, pst_recv), (pair2_send, pair2_recv))[which]
        return remote(src.at[p], dst.at[p], pr_send.at[which, p], pr_recv.at[which, p], partner)

    def chip_copy(which, p, slot):
        src, dst = ((chip_send, chip_recv), (cst_send, cst_recv), (chip2_send, chip2_recv))[which]
        return remote(
            src.at[p], dst.at[slot], ch_send.at[which, p], ch_recv.at[which, slot], 2 * p + core
        )

    def to_pair(j):
        p = lax.rem(chip + 1 + j, half)
        d = 2 * p + 1 - core
        pst_send[p] = stats[slab(d), :]
        pair_copy(1, p).start()
        pair_send[p] = part[:, slab(d), :].astype(bf16)
        pair_copy(0, p).start()

    loop(0, half, to_pair)

    def merge(p):
        d = 2 * p + core
        pair_copy(1, p).wait_recv()
        s1, s2 = stats[slab(d), :], pst_recv[p]
        m = jnp.maximum(s1, s2)
        a1, a2 = jnp.exp(s1 - m), jnp.exp(s2 - m)
        t = s1 * pltpu.roll(a1, 64, 1) + s2 * pltpu.roll(a2, 64, 1)
        pair_copy(0, p).wait_recv()
        summed = part[:, slab(d), :] * columns_of(a1) + pair_recv[p].astype(f32) * columns_of(a2)
        return jnp.where(small < 64, m, t), summed.astype(bf16)

    def to_owner(j):
        p = lax.rem(chip + 1 + j, half)
        state, summed = merge(p)
        cst_send[p] = state
        chip_copy(1, p, chip).start()
        chip_send[p] = summed
        chip_copy(0, p, chip).start()

    loop(0, half - 1, to_owner)
    state, summed = merge(chip)
    cst_recv[chip] = state
    chip_recv[chip] = summed

    def settle(which):
        def body(k):
            p = lax.rem(chip + half - k, half)
            chip_copy(which, p, p).wait_recv()

        return body

    loop(1, half, settle(1))
    loop(1, half, settle(0))
    peak = jnp.max(cst_recv[...], axis=0)

    def add(p, carry):
        totals, acc = carry
        s = cst_recv[p]
        a = jnp.exp(s - peak)
        totals = totals + s * pltpu.roll(a, 64, 1)
        return totals, acc + chip_recv[p].astype(f32) * columns_of(a)

    totals, acc = lax.fori_loop(
        0, half, add,
        (jnp.zeros((chunk, HEAD_SIZE), f32), jnp.zeros((KEY_VALUE_HEADS, chunk, HEAD_SIZE), f32)),
    )
    wide = (acc / columns_of(totals, 64)).astype(bf16).astype(f32)
    squares = jnp.sum(jnp.sum(wide * wide, axis=0), axis=1, keepdims=True)
    features = KEY_VALUE_HEADS * GROUP * HEAD_SIZE
    scale = jnp.concatenate(
        [
            jnp.broadcast_to(
                lax.rsqrt(
                    jnp.sum(squares[r * GROUP : (r + 1) * GROUP], axis=0, keepdims=True) / features
                    + EPS
                ),
                (GROUP, HEAD_SIZE),
            )
            for r in range(rows)
        ],
        axis=0,
    )
    gain = jnp.concatenate([gain_ref[...]] * rows, axis=1)
    gathx[me] = (wide * scale[None] * gain).astype(bf16)

    def finish_sends(which):
        loop(0, half, lambda p: pair_copy(which, p).wait_send())
        loop(1, half, lambda k: chip_copy(which, lax.rem(chip + k, half), chip).wait_send())

    gather(gathx, 1, lambda: (finish_sends(0), finish_sends(1)))

    def widen(d):
        part[:, slab(d), :] = gathx[d].astype(f32)

    loop(0, n, widen)

    def spread(g):
        for h in range(GROUP):
            span = pl.ds(pl.multiple_of((g * GROUP + h) * HEAD_SIZE, HEAD_SIZE), HEAD_SIZE)
            xs[:, span] = part[g, pl.ds(h, n * rows, stride=GROUP), :].astype(bf16)

    loop(0, KEY_VALUE_HEADS, spread)

    for copy in w_copies[: 2 * PIECES]:
        copy.wait()
    first = 0
    while first < hidden:
        size = min(256, hidden - first)
        contract = (((1,), (1,)), ((), ()))
        gate = lax.dot_general(xs[...], wg[first : first + size, :], contract, preferred_element_type=f32)
        up = lax.dot_general(xs[...], wu[first : first + size, :], contract, preferred_element_type=f32)
        act[:, first : first + size] = (gate / (1.0 + jnp.exp(-gate)) * up).astype(bf16)
        first += size
    for copy in w_copies[2 * PIECES :]:
        copy.wait()

    def down(g):
        width = GROUP * HEAD_SIZE
        o = jnp.dot(
            act[...], wd[:, pl.ds(pl.multiple_of(g * width, width), width)],
            preferred_element_type=f32,
        )
        for h in range(GROUP):
            part[g, pl.ds(h, n * rows, stride=GROUP), :] = o[:, h * HEAD_SIZE : (h + 1) * HEAD_SIZE]

    loop(0, KEY_VALUE_HEADS, down)

    def to_pair2(j):
        p = lax.rem(chip + 1 + j, half)
        pair2_send[p] = part[:, slab(2 * p + 1 - core), :].astype(bf16)
        pair_copy(2, p).start()

    loop(0, half, to_pair2)

    def merge2(p):
        pair_copy(2, p).wait_recv()
        return part[:, slab(2 * p + core), :] + pair2_recv[p].astype(f32)

    def to_owner2(j):
        p = lax.rem(chip + 1 + j, half)
        chip2_send[p] = merge2(p).astype(bf16)
        chip_copy(2, p, chip).start()

    loop(0, half - 1, to_owner2)
    mine = merge2(chip)

    def add2(k, acc):
        p = lax.rem(chip + half - k, half)
        chip_copy(2, p, p).wait_recv()
        return acc + chip2_recv[p].astype(f32)

    out_ref[...] = lax.fori_loop(1, half, add2, mine).astype(bf16)
    finish_sends(2)


def local(queries, keys, values, position, lengths, gain, gate_weight, up_weight, down_weight):
    n = lax.axis_size("ctx")
    half = n // 2
    rows, width = queries.shape
    slots, kv_width = keys.shape
    hidden = gate_weight.shape[0]
    chunk = rows * GROUP
    q = queries.reshape(rows, KEY_VALUE_HEADS, GROUP, HEAD_SIZE).transpose(1, 0, 2, 3)
    q = q.reshape(KEY_VALUE_HEADS, chunk, HEAD_SIZE)
    spread = jnp.broadcast_to(lengths[:, None, None], (rows, GROUP, 64)).reshape(1, chunk, 64)
    coded = jnp.concatenate([spread // 256, spread % 256], axis=2).astype(bf16)
    q = jnp.concatenate([q, coded], axis=0)

    block = (KEY_VALUE_HEADS, chunk, HEAD_SIZE)
    vm = pltpu.VMEM
    data = lambda: vm((half,) + block, bf16)
    state = lambda: vm((half, chunk, HEAD_SIZE), f32)
    dma = pltpu.SemaphoreType.DMA
    in_vmem = pl.BlockSpec(memory_space=pltpu.VMEM)
    in_hbm = pl.BlockSpec(memory_space=pl.ANY)
    out = pl.pallas_call(
        functools.partial(kernel, n, rows),
        out_shape=jax.ShapeDtypeStruct(block, bf16),
        in_specs=[in_vmem] * 3 + [in_hbm] * 5,
        out_specs=in_vmem,
        scratch_shapes=[
            vm((slots, kv_width), bf16),
            vm((slots, kv_width), bf16),
            vm((hidden, width), bf16),
            vm((hidden, width), bf16),
            vm((hidden, width), bf16),
            vm((n, KEY_VALUE_HEADS + 1, chunk, HEAD_SIZE), bf16),
            vm((n,) + block, bf16),
            vm((KEY_VALUE_HEADS, n * chunk, HEAD_SIZE), f32),
            vm((n * chunk, HEAD_SIZE), f32),
            vm((n * rows, width), bf16),
            vm((n * rows, hidden), bf16),
            data(), data(), state(), state(),
            data(), data(), state(), state(),
            data(), data(), data(), data(),
            dma((2,)), dma((3, PIECES)),
            dma((2, half)), dma((2, half)), dma((2, n)),
            dma((3, half)), dma((3, half)), dma((3, half)), dma((3, half)),
        ],
        compiler_params=pltpu.CompilerParams(
            collective_id=0, has_side_effects=True, vmem_limit_bytes=60 * 2**20
        ),
    )(
        q, position.reshape(1, slots), gain.reshape(KEY_VALUE_HEADS, GROUP, HEAD_SIZE),
        keys, values, gate_weight, up_weight, down_weight,
    )
    out = out.reshape(KEY_VALUE_HEADS, rows, GROUP, HEAD_SIZE).transpose(1, 0, 2, 3)
    return out.reshape(rows, width)


def solution(mesh):
    split = P(("groups", "ctx"))
    tall = P(("groups", "ctx"), None)
    weight = P("ctx", None)
    return jax.shard_map(
        local,
        mesh=mesh,
        in_specs=(tall, tall, tall, split, split, P(), weight, weight, weight),
        out_specs=tall,
        check_vma=False,
    )
```

```python
import functools

import jax
import jax.numpy as jnp
from jax import lax
from jax.experimental import pallas as pl
from jax.experimental.pallas import tpu as pltpu
from jax.sharding import PartitionSpec as P

KEY_VALUE_HEADS = 8
GROUP = 8
HEAD_SIZE = 128
EPS = 1e-5
PIECES = 4
MESH = pl.DeviceIdType.MESH
bf16, f32 = jnp.bfloat16, jnp.float32


def kernel(
    n, rows, len_ref, q_ref, pos_ref, gain_ref, k_hbm, v_hbm, wg_hbm, wu_hbm, wd_hbm, out_ref,
    k_v, v_v, wg, wu, wd, gathq, gathx, part, stats, square, gate_sum, up_sum, act, turn,
    pair_send, pair_recv, pst_send, pst_recv, chip_send, chip_recv, cst_send, cst_recv,
    pair2_send, pair2_recv, chip2_send, chip2_recv,
    load_sem, w_sem, ag_send, ag_fwd, ag_recv, pr_send, pr_recv, ch_send, ch_recv,
):
    me = lax.axis_index("ctx")
    half = n // 2
    core = lax.rem(me, 2)
    chip = me // 2
    partner = me + 1 - 2 * core
    chunk = rows * GROUP
    hidden = wg.shape[0]

    k_copy = pltpu.make_async_copy(k_hbm, k_v, load_sem.at[0])
    v_copy = pltpu.make_async_copy(v_hbm, v_v, load_sem.at[1])
    k_copy.start()
    v_copy.start()
    w_copies = []
    step = hidden // PIECES // 16 * 16
    for i, (src, dst) in enumerate(((wg_hbm, wg), (wu_hbm, wu), (wd_hbm, wd))):
        for j in range(PIECES):
            size = step if j < PIECES - 1 else hidden - step * (PIECES - 1)
            span = pl.ds(j * step, size)
            w_copies.append(
                pltpu.make_async_copy(src.at[span], dst.at[span], w_sem.at[i, j])
            )

    def remote(src, dst, send, recv, to):
        return pltpu.make_async_remote_copy(
            src_ref=src, dst_ref=dst, send_sem=send, recv_sem=recv,
            device_id={"ctx": to}, device_id_type=MESH,
        )

    def loop(lo, hi, body):
        def step(i, carry):
            body(i)
            return carry

        lax.fori_loop(lo, hi, step, 0)

    barrier = pltpu.get_barrier_semaphore()
    pl.semaphore_signal(barrier, inc=1, device_id={"ctx": partner}, device_id_type=MESH)

    def greet(k):
        to = 2 * lax.rem(chip + k, half) + core
        pl.semaphore_signal(barrier, inc=1, device_id={"ctx": to}, device_id_type=MESH)

    loop(1, half, greet)
    q = q_ref[...].astype(f32)
    for g in range(KEY_VALUE_HEADS):
        for h in range(GROUP):
            first = (g * GROUP + h) * HEAD_SIZE
            turn[g, pl.ds(h, rows, stride=GROUP), :] = q[:, first : first + HEAD_SIZE]
    gathq[me, :KEY_VALUE_HEADS] = turn[...].astype(bf16)
    low = lax.broadcasted_iota(jnp.int32, (GROUP, HEAD_SIZE), 1) < 64
    coded = [jnp.where(low, len_ref[r] >> 8, len_ref[r] & 255) for r in range(rows)]
    gathq[me, KEY_VALUE_HEADS] = jnp.concatenate(coded, axis=0).astype(f32).astype(bf16)
    pl.semaphore_wait(barrier, half)

    def gather_copy(which, source, to, send):
        buf = (gathq, gathx)[which]
        return remote(buf.at[source], buf.at[source], send, ag_recv.at[which, source], to)

    def source_of(k):
        return lax.rem(chip + half - k, half)

    def gather_start(which):
        def send(k):
            to = 2 * lax.rem(chip + k, half) + core
            gather_copy(which, me, to, ag_send.at[which, k]).start()

        gather_copy(which, me, partner, ag_send.at[which, 0]).start()
        loop(1, half, send)

    def forward(which, k):
        source = 2 * source_of(k) + core
        gather_copy(which, source, partner, ag_fwd.at[which, k]).wait_recv()
        gather_copy(which, source, partner, ag_fwd.at[which, k]).start()

    def arrive(which, p):
        gather_copy(which, 2 * p + 1 - core, partner, ag_send.at[which, 0]).wait_recv()

    def gather_end(which):
        loop(0, half, lambda k: gather_copy(which, me, partner, ag_send.at[which, k]).wait_send())

        def forwarded(k):
            source = 2 * source_of(k) + core
            gather_copy(which, source, partner, ag_fwd.at[which, k]).wait_send()

        loop(1, half, forwarded)

    gather_start(0)
    for copy in w_copies:
        copy.start()
    loop(1, half, lambda k: forward(0, k))
    loop(0, half, lambda p: arrive(0, p))

    def slab(d):
        return pl.ds(pl.multiple_of(d * chunk, chunk), chunk)

    every = n * rows
    own_heads = KEY_VALUE_HEADS * GROUP // n
    block = own_heads * every
    shared = half // KEY_VALUE_HEADS

    def widen(d):
        part[:, slab(d), :] = gathq[d, :KEY_VALUE_HEADS].astype(f32)
        stats[0, slab(d), :] = gathq[d, KEY_VALUE_HEADS].astype(f32)

    loop(0, n, widen)
    limits = stats[0, pl.ds(0, every, stride=GROUP), :]
    limit = jnp.concatenate([limits[:, 0:1] * 256.0 + limits[:, 64:65]] * GROUP, axis=0)
    live = pos_ref[...].astype(f32) < limit
    lane = lax.broadcasted_iota(jnp.int32, (GROUP * every, HEAD_SIZE), 1)
    small = lax.broadcasted_iota(jnp.int32, (block, HEAD_SIZE), 1)
    k_copy.wait()
    v_copy.wait()

    def pair_copy(which, p):
        src, dst = ((pair_send, pair_recv), (pst_send, pst_recv), (pair2_send, pair2_recv))[which]
        return remote(src.at[p], dst.at[p], pr_send.at[which, p], pr_recv.at[which, p], partner)

    def chip_copy(which, p, slot):
        src, dst = ((chip_send, chip_recv), (cst_send, cst_recv), (chip2_send, chip2_recv))[which]
        return remote(
            src.at[p], dst.at[slot], ch_send.at[which, p], ch_recv.at[which, slot], 2 * p + core
        )

    def head_at(j):
        return lax.rem(chip // shared + 1 + j, KEY_VALUE_HEADS)

    def rows_of(i):
        return pl.ds(pl.multiple_of(i * block, block), block)

    def merge(j):
        g = head_at(j)
        for i in range(shared):
            p = g * shared + i
            span = rows_of(2 * i + core)
            pair_copy(1, p).wait_recv()
            theirs = jnp.transpose(pst_recv[p])
            m1, t1 = stats[g, span, 0:1], stats[g, span, 4:5]
            m2, t2 = theirs[:, 0:1], theirs[:, 4:5]
            m = jnp.maximum(m1, m2)
            a1, a2 = jnp.exp(m1 - m), jnp.exp(m2 - m)
            state = jnp.transpose(jnp.where(small < 4, m, t1 * a1 + t2 * a2))[0:8]
            pair_copy(0, p).wait_recv()
            summed = (part[g, span, :] * a1 + pair_recv[p].astype(f32) * a2).astype(bf16)

            @pl.when(p == chip)
            def _():
                cst_recv[chip] = state
                chip_recv[chip] = summed

            @pl.when(p != chip)
            def _():
                cst_send[p] = state
                chip_copy(1, p, chip).start()
                chip_send[p] = summed
                chip_copy(0, p, chip).start()

    def head(j):
        g = head_at(j)
        span = pl.ds(pl.multiple_of(g * HEAD_SIZE, HEAD_SIZE), HEAD_SIZE)
        q = jnp.concatenate(
            [part[g, pl.ds(h, every, stride=GROUP), :] for h in range(GROUP)], axis=0
        ).astype(bf16)
        s = lax.dot_general(
            q, k_v[:, span], (((1,), (1,)), ((), ())), preferred_element_type=f32
        ) * HEAD_SIZE ** (-0.5)
        s = jnp.where(live, s, -1e30)
        m = jnp.max(s, axis=1, keepdims=True)
        w = jnp.where(live, jnp.exp(s - m), 0.0)
        t = jnp.sum(w, axis=1, keepdims=True)
        part[g] = jnp.dot(w.astype(bf16), v_v[:, span], preferred_element_type=f32)
        stats[g] = jnp.where(lane < 4, m, t)
        for i in range(shared):
            p = g * shared + i
            theirs = rows_of(2 * i + 1 - core)
            pst_send[p] = jnp.transpose(stats[g, theirs, :])[0:8]
            pair_copy(1, p).start()
            pair_send[p] = part[g, theirs, :].astype(bf16)
            pair_copy(0, p).start()

        @pl.when(j > 0)
        def _():
            merge(j - 1)

    loop(0, KEY_VALUE_HEADS, head)
    merge(KEY_VALUE_HEADS - 1)

    def settle(k):
        p = source_of(k)
        chip_copy(1, p, p).wait_recv()
        chip_copy(0, p, p).wait_recv()

    loop(1, half, settle)
    peaks, totals = cst_recv[:, 0, :], cst_recv[:, 4, :]
    factor = jnp.exp(peaks - jnp.max(peaks, axis=0, keepdims=True))
    factor = factor / jnp.sum(factor * totals, axis=0, keepdims=True)
    factor = jnp.transpose(factor)
    attended = jnp.zeros((block, HEAD_SIZE), f32)
    for p in range(half):
        attended = attended + chip_recv[p].astype(f32) * factor[:, p : p + 1]
    attended = attended.astype(bf16)
    gathx[me] = jnp.concatenate(
        [attended[i * every : (i + 1) * every] for i in range(own_heads)], axis=1
    )

    def finish_sends(which):
        loop(0, half, lambda p: pair_copy(which, p).wait_send())
        loop(1, half, lambda k: chip_copy(which, lax.rem(chip + k, half), chip).wait_send())

    gather_start(1)
    gather_end(0)
    finish_sends(0)
    finish_sends(1)
    for copy in w_copies[: 2 * PIECES]:
        copy.wait()
    square[...] = jnp.zeros_like(square)
    gate_sum[...] = jnp.zeros_like(gate_sum)
    up_sum[...] = jnp.zeros_like(up_sum)
    deep = 2 * own_heads * HEAD_SIZE

    def products(p):
        x = jnp.concatenate([gathx[2 * p], gathx[2 * p + 1]], axis=1).astype(f32)
        span = pl.ds(pl.multiple_of(p * deep, deep), deep)
        total = square[...]
        for i in range(2 * own_heads):
            piece = x[:, i * HEAD_SIZE : (i + 1) * HEAD_SIZE]
            total = total + piece * piece
        square[...] = total
        scaled = (x * gain_ref[:, span]).astype(bf16)
        contract = (((1,), (1,)), ((), ()))
        first = 0
        while first < hidden:
            size = min(256, hidden - first)
            cut = slice(first, first + size)
            gate_sum[:, cut] += lax.dot_general(
                scaled, wg[cut, span], contract, preferred_element_type=f32
            )
            up_sum[:, cut] += lax.dot_general(
                scaled, wu[cut, span], contract, preferred_element_type=f32
            )
            first += size

    forward(1, 1)
    arrive(1, chip)
    products(chip)

    def next_chip(k):
        @pl.when(k + 1 < half)
        def _():
            forward(1, k + 1)

        arrive(1, source_of(k))
        products(source_of(k))

    loop(1, half, next_chip)
    features = KEY_VALUE_HEADS * GROUP * HEAD_SIZE
    scale = lax.rsqrt(jnp.sum(square[...], axis=1, keepdims=True) / features + EPS)
    gate = gate_sum[...] * scale
    act[...] = (gate / (1.0 + jnp.exp(-gate)) * (up_sum[...] * scale)).astype(bf16)
    gather_end(1)
    for copy in w_copies[2 * PIECES :]:
        copy.wait()

    def down(g):
        width = GROUP * HEAD_SIZE
        o = jnp.dot(
            act[...], wd[:, pl.ds(pl.multiple_of(g * width, width), width)],
            preferred_element_type=f32,
        )
        for h in range(GROUP):
            part[g, pl.ds(h, n * rows, stride=GROUP), :] = o[:, h * HEAD_SIZE : (h + 1) * HEAD_SIZE]

    loop(0, KEY_VALUE_HEADS, down)

    def to_pair2(j):
        p = lax.rem(chip + 1 + j, half)
        pair2_send[p] = part[:, slab(2 * p + 1 - core), :].astype(bf16)
        pair_copy(2, p).start()

    loop(0, half, to_pair2)

    def merge2(p):
        pair_copy(2, p).wait_recv()
        return part[:, slab(2 * p + core), :] + pair2_recv[p].astype(f32)

    def to_owner2(j):
        p = lax.rem(chip + 1 + j, half)
        chip2_send[p] = merge2(p).astype(bf16)
        chip_copy(2, p, chip).start()

    loop(0, half - 1, to_owner2)
    mine = merge2(chip)

    def add2(k, acc):
        p = lax.rem(chip + half - k, half)
        chip_copy(2, p, p).wait_recv()
        return acc + chip2_recv[p].astype(f32)

    turn[...] = lax.fori_loop(1, half, add2, mine)
    out_ref[...] = jnp.concatenate(
        [
            turn[g, pl.ds(h, rows, stride=GROUP), :]
            for g in range(KEY_VALUE_HEADS)
            for h in range(GROUP)
        ],
        axis=1,
    ).astype(bf16)
    finish_sends(2)


def local(queries, keys, values, position, lengths, gain, gate_weight, up_weight, down_weight):
    n = lax.axis_size("ctx")
    half = n // 2
    rows, width = queries.shape
    slots, kv_width = keys.shape
    hidden = gate_weight.shape[0]
    chunk = rows * GROUP
    own = KEY_VALUE_HEADS * GROUP // n
    every = n * rows
    block = (KEY_VALUE_HEADS, chunk, HEAD_SIZE)
    vm = pltpu.VMEM
    data = lambda: vm((half,) + block, bf16)
    state = lambda: vm((half, 8, HEAD_SIZE), f32)
    heads = lambda: vm((half, own * every, HEAD_SIZE), bf16)
    dma = pltpu.SemaphoreType.DMA
    in_vmem = pl.BlockSpec(memory_space=pltpu.VMEM)
    in_hbm = pl.BlockSpec(memory_space=pl.ANY)
    return pl.pallas_call(
        functools.partial(kernel, n, rows),
        out_shape=jax.ShapeDtypeStruct((rows, width), bf16),
        in_specs=[pl.BlockSpec(memory_space=pltpu.SMEM)] + [in_vmem] * 3 + [in_hbm] * 5,
        out_specs=in_vmem,
        scratch_shapes=[
            vm((slots, kv_width), bf16),
            vm((slots, kv_width), bf16),
            vm((hidden, width), bf16),
            vm((hidden, width), bf16),
            vm((hidden, width), bf16),
            vm((n, KEY_VALUE_HEADS + 1, chunk, HEAD_SIZE), bf16),
            vm((n, every, own * HEAD_SIZE), bf16),
            vm((KEY_VALUE_HEADS, n * chunk, HEAD_SIZE), f32),
            vm((KEY_VALUE_HEADS, n * chunk, HEAD_SIZE), f32),
            vm((every, HEAD_SIZE), f32),
            vm((every, hidden), f32),
            vm((every, hidden), f32),
            vm((every, hidden), bf16),
            vm(block, f32),
            heads(), heads(), state(), state(),
            heads(), heads(), state(), state(),
            data(), data(), data(), data(),
            dma((2,)), dma((3, PIECES)),
            dma((2, half)), dma((2, half)), dma((2, n)),
            dma((3, half)), dma((3, half)), dma((3, half)), dma((3, half)),
        ],
        compiler_params=pltpu.CompilerParams(
            collective_id=0, has_side_effects=True, vmem_limit_bytes=60 * 2**20
        ),
    )(
        lengths, queries, position.reshape(1, slots), gain.reshape(1, width),
        keys, values, gate_weight, up_weight, down_weight,
    )


def solution(mesh):
    split = P(("groups", "ctx"))
    tall = P(("groups", "ctx"), None)
    weight = P("ctx", None)
    return jax.shard_map(
        local,
        mesh=mesh,
        in_specs=(tall, tall, tall, split, split, P(), weight, weight, weight),
        out_specs=tall,
        check_vma=False,
    )
```

```python
import functools

import jax
import jax.numpy as jnp
from jax import lax
from jax.experimental import pallas as pl
from jax.experimental.pallas import tpu as pltpu
from jax.sharding import PartitionSpec as P

KEY_VALUE_HEADS = 8
GROUP = 8
HEAD_SIZE = 128
EPS = 1e-5
PIECES = 4
MESH = pl.DeviceIdType.MESH
bf16, f32 = jnp.bfloat16, jnp.float32


def kernel(
    n, rows, len_ref, q_ref, pos_ref, gain_ref, k_hbm, v_hbm, wg_hbm, wu_hbm, wd_hbm, out_ref,
    k_v, v_v, wg, wu, wd, gathq, gathx, part, stats, square, gate_sum, up_sum, act, turn,
    pair_send, pair_recv, pst_send, pst_recv, chip_send, chip_recv, cst_send, cst_recv,
    pair2_send, pair2_recv, chip2_send, chip2_recv,
    load_sem, w_sem, ag_send, ag_fwd, ag_side, ag_recv, pr_send, pr_recv, ch_send, ch_recv,
):
    me = lax.axis_index("ctx")
    half = n // 2
    core = lax.rem(me, 2)
    chip = me // 2
    partner = me + 1 - 2 * core
    chunk = rows * GROUP
    hidden = wg.shape[0]

    k_copy = pltpu.make_async_copy(k_hbm, k_v, load_sem.at[0])
    v_copy = pltpu.make_async_copy(v_hbm, v_v, load_sem.at[1])
    k_copy.start()
    v_copy.start()
    w_copies = []
    step = hidden // PIECES // 16 * 16
    for i, (src, dst) in enumerate(((wg_hbm, wg), (wu_hbm, wu), (wd_hbm, wd))):
        for j in range(PIECES):
            size = step if j < PIECES - 1 else hidden - step * (PIECES - 1)
            span = pl.ds(j * step, size)
            w_copies.append(
                pltpu.make_async_copy(src.at[span], dst.at[span], w_sem.at[i, j])
            )

    def remote(src, dst, send, recv, to):
        return pltpu.make_async_remote_copy(
            src_ref=src, dst_ref=dst, send_sem=send, recv_sem=recv,
            device_id={"ctx": to}, device_id_type=MESH,
        )

    def loop(lo, hi, body):
        def step(i, carry):
            body(i)
            return carry

        lax.fori_loop(lo, hi, step, 0)

    barrier = pltpu.get_barrier_semaphore()
    pl.semaphore_signal(barrier, inc=1, device_id={"ctx": partner}, device_id_type=MESH)

    def greet(k):
        to = 2 * lax.rem(chip + k, half) + core
        pl.semaphore_signal(barrier, inc=1, device_id={"ctx": to}, device_id_type=MESH)

    loop(1, half, greet)
    q = q_ref[...].astype(f32)
    for g in range(KEY_VALUE_HEADS):
        for h in range(GROUP):
            first = (g * GROUP + h) * HEAD_SIZE
            turn[g, pl.ds(h, rows, stride=GROUP), :] = q[:, first : first + HEAD_SIZE]
    gathq[me, :KEY_VALUE_HEADS] = turn[...].astype(bf16)
    low = lax.broadcasted_iota(jnp.int32, (GROUP, HEAD_SIZE), 1) < 64
    coded = [jnp.where(low, len_ref[r] >> 8, len_ref[r] & 255) for r in range(rows)]
    gathq[me, KEY_VALUE_HEADS] = jnp.concatenate(coded, axis=0).astype(f32).astype(bf16)
    pl.semaphore_wait(barrier, half)

    def gather_copy(which, source, to, send):
        buf = (gathq, gathx)[which]
        return remote(buf.at[source], buf.at[source], send, ag_recv.at[which, source], to)

    twos = half // 2
    two, side = chip // 2, lax.rem(chip, 2)
    beside = 2 * (chip + 1 - 2 * side) + core

    def source_of(i):
        other = lax.rem(i, 2)
        return 2 * lax.rem(two + twos - i // 2, twos) + side + other * (1 - 2 * side)

    def gather_start(which):
        def send(k):
            to = 2 * (2 * lax.rem(two + k, twos) + side) + core
            gather_copy(which, me, to, ag_send.at[which, k]).start()

        loop(1, twos, send)
        gather_copy(which, me, beside, ag_send.at[which, twos]).start()
        gather_copy(which, me, partner, ag_send.at[which, 0]).start()

    def forward(which, i):
        source = 2 * source_of(i) + core
        gather_copy(which, source, partner, ag_fwd.at[which, i]).wait_recv()

        @pl.when(lax.rem(i, 2) == 0)
        def _():
            gather_copy(which, source, beside, ag_side.at[which, i // 2]).start()

        gather_copy(which, source, partner, ag_fwd.at[which, i]).start()

    def arrive(which, p):
        gather_copy(which, 2 * p + 1 - core, partner, ag_send.at[which, 0]).wait_recv()

    def gather_end(which):
        def sent(sems):
            return lambda k: gather_copy(which, me, partner, sems.at[which, k]).wait_send()

        loop(0, twos + 1, sent(ag_send))
        loop(1, half, sent(ag_fwd))
        loop(1, twos, sent(ag_side))

    gather_start(0)
    for copy in w_copies:
        copy.start()
    loop(1, half, lambda k: forward(0, k))
    loop(0, half, lambda p: arrive(0, p))

    def slab(d):
        return pl.ds(pl.multiple_of(d * chunk, chunk), chunk)

    every = n * rows
    own_heads = KEY_VALUE_HEADS * GROUP // n
    block = own_heads * every
    shared = half // KEY_VALUE_HEADS

    def widen(d):
        part[:, slab(d), :] = gathq[d, :KEY_VALUE_HEADS].astype(f32)
        stats[0, slab(d), :] = gathq[d, KEY_VALUE_HEADS].astype(f32)

    loop(0, n, widen)
    limits = stats[0, pl.ds(0, every, stride=GROUP), :]
    limit = jnp.concatenate([limits[:, 0:1] * 256.0 + limits[:, 64:65]] * GROUP, axis=0)
    live = pos_ref[...].astype(f32) < limit
    lane = lax.broadcasted_iota(jnp.int32, (GROUP * every, HEAD_SIZE), 1)
    small = lax.broadcasted_iota(jnp.int32, (block, HEAD_SIZE), 1)
    k_copy.wait()
    v_copy.wait()

    def pair_copy(which, p):
        if which >= 2:
            part_of = pl.ds((which - 2) * KEY_VALUE_HEADS // 2, KEY_VALUE_HEADS // 2)
            src, dst = pair2_send.at[p, part_of], pair2_recv.at[p, part_of]
            return remote(src, dst, pr_send.at[which, p], pr_recv.at[which, p], partner)
        src, dst = ((pair_send, pair_recv), (pst_send, pst_recv))[which]
        return remote(src.at[p], dst.at[p], pr_send.at[which, p], pr_recv.at[which, p], partner)

    def chip_copy(which, p, slot):
        if which >= 2:
            part_of = pl.ds((which - 2) * KEY_VALUE_HEADS // 2, KEY_VALUE_HEADS // 2)
            src, dst = chip2_send.at[p, part_of], chip2_recv.at[slot, part_of]
            return remote(
                src, dst, ch_send.at[which, p], ch_recv.at[which, slot], 2 * p + core
            )
        src, dst = ((chip_send, chip_recv), (cst_send, cst_recv))[which]
        return remote(
            src.at[p], dst.at[slot], ch_send.at[which, p], ch_recv.at[which, slot], 2 * p + core
        )

    def head_at(j):
        return lax.rem(chip // shared + 1 + j, KEY_VALUE_HEADS)

    def rows_of(i):
        return pl.ds(pl.multiple_of(i * block, block), block)

    def merge(j):
        g = head_at(j)
        for i in range(shared):
            p = g * shared + i
            span = rows_of(2 * i + core)
            pair_copy(1, p).wait_recv()
            theirs = jnp.transpose(pst_recv[p])
            m1, t1 = stats[g, span, 0:1], stats[g, span, 4:5]
            m2, t2 = theirs[:, 0:1], theirs[:, 4:5]
            m = jnp.maximum(m1, m2)
            a1, a2 = jnp.exp(m1 - m), jnp.exp(m2 - m)
            state = jnp.transpose(jnp.where(small < 4, m, t1 * a1 + t2 * a2))[0:8]
            pair_copy(0, p).wait_recv()
            summed = (part[g, span, :] * a1 + pair_recv[p].astype(f32) * a2).astype(bf16)

            @pl.when(p == chip)
            def _():
                cst_recv[chip] = state
                chip_recv[chip] = summed

            @pl.when(p != chip)
            def _():
                cst_send[p] = state
                chip_copy(1, p, chip).start()
                chip_send[p] = summed
                chip_copy(0, p, chip).start()

    def head(j):
        g = head_at(j)
        span = pl.ds(pl.multiple_of(g * HEAD_SIZE, HEAD_SIZE), HEAD_SIZE)
        q = jnp.concatenate(
            [part[g, pl.ds(h, every, stride=GROUP), :] for h in range(GROUP)], axis=0
        ).astype(bf16)
        s = lax.dot_general(
            q, k_v[:, span], (((1,), (1,)), ((), ())), preferred_element_type=f32
        ) * HEAD_SIZE ** (-0.5)
        s = jnp.where(live, s, -1e30)
        m = jnp.max(s, axis=1, keepdims=True)
        w = jnp.where(live, jnp.exp(s - m), 0.0)
        t = jnp.sum(w, axis=1, keepdims=True)
        part[g] = jnp.dot(w.astype(bf16), v_v[:, span], preferred_element_type=f32)
        stats[g] = jnp.where(lane < 4, m, t)
        for i in range(shared):
            p = g * shared + i
            theirs = rows_of(2 * i + 1 - core)
            pst_send[p] = jnp.transpose(stats[g, theirs, :])[0:8]
            pair_copy(1, p).start()
            pair_send[p] = part[g, theirs, :].astype(bf16)
            pair_copy(0, p).start()

        @pl.when(j > 0)
        def _():
            merge(j - 1)

    loop(0, KEY_VALUE_HEADS, head)
    merge(KEY_VALUE_HEADS - 1)

    def settle(k):
        p = source_of(k)
        chip_copy(1, p, p).wait_recv()
        chip_copy(0, p, p).wait_recv()

    loop(1, half, settle)
    peaks, totals = cst_recv[:, 0, :], cst_recv[:, 4, :]
    factor = jnp.exp(peaks - jnp.max(peaks, axis=0, keepdims=True))
    factor = factor / jnp.sum(factor * totals, axis=0, keepdims=True)
    factor = jnp.transpose(factor)
    attended = jnp.zeros((block, HEAD_SIZE), f32)
    for p in range(half):
        attended = attended + chip_recv[p].astype(f32) * factor[:, p : p + 1]
    attended = attended.astype(bf16)
    gathx[me] = jnp.concatenate(
        [attended[i * every : (i + 1) * every] for i in range(own_heads)], axis=1
    )

    def finish_sends(which):
        loop(0, half, lambda p: pair_copy(which, p).wait_send())
        loop(1, half, lambda k: chip_copy(which, lax.rem(chip + k, half), chip).wait_send())

    gather_start(1)
    gather_end(0)
    finish_sends(0)
    finish_sends(1)
    for copy in w_copies[: 2 * PIECES]:
        copy.wait()
    square[...] = jnp.zeros_like(square)
    gate_sum[...] = jnp.zeros_like(gate_sum)
    up_sum[...] = jnp.zeros_like(up_sum)
    deep = 2 * own_heads * HEAD_SIZE

    def products(p):
        x = jnp.concatenate([gathx[2 * p], gathx[2 * p + 1]], axis=1).astype(f32)
        span = pl.ds(pl.multiple_of(p * deep, deep), deep)
        total = square[...]
        for i in range(2 * own_heads):
            piece = x[:, i * HEAD_SIZE : (i + 1) * HEAD_SIZE]
            total = total + piece * piece
        square[...] = total
        scaled = (x * gain_ref[:, span]).astype(bf16)
        contract = (((1,), (1,)), ((), ()))
        first = 0
        while first < hidden:
            size = min(256, hidden - first)
            cut = slice(first, first + size)
            gate_sum[:, cut] += lax.dot_general(
                scaled, wg[cut, span], contract, preferred_element_type=f32
            )
            up_sum[:, cut] += lax.dot_general(
                scaled, wu[cut, span], contract, preferred_element_type=f32
            )
            first += size

    forward(1, 1)
    forward(1, 2)
    arrive(1, chip)
    products(chip)

    def next_chip(k):
        @pl.when(k + 2 < half)
        def _():
            forward(1, k + 2)

        arrive(1, source_of(k))
        products(source_of(k))

    loop(1, half, next_chip)
    features = KEY_VALUE_HEADS * GROUP * HEAD_SIZE
    scale = lax.rsqrt(jnp.sum(square[...], axis=1, keepdims=True) / features + EPS)
    gate = gate_sum[...] * scale
    act[...] = (gate / (1.0 + jnp.exp(-gate)) * (up_sum[...] * scale)).astype(bf16)
    gather_end(1)
    for copy in w_copies[2 * PIECES :]:
        copy.wait()

    def down(g):
        width = GROUP * HEAD_SIZE
        o = jnp.dot(
            act[...], wd[:, pl.ds(pl.multiple_of(g * width, width), width)],
            preferred_element_type=f32,
        )
        for h in range(GROUP):
            part[g, pl.ds(h, n * rows, stride=GROUP), :] = o[:, h * HEAD_SIZE : (h + 1) * HEAD_SIZE]

    middle = KEY_VALUE_HEADS // 2

    def to_pair2(i):
        heads = pl.ds(i * middle, middle)

        def body(j):
            p = lax.rem(chip + 1 + j, half)
            pair2_send[p, heads] = part[heads, slab(2 * p + 1 - core), :].astype(bf16)
            pair_copy(2 + i, p).start()

        loop(0, half, body)

    def merge2(i, p):
        heads = pl.ds(i * middle, middle)
        pair_copy(2 + i, p).wait_recv()
        return part[heads, slab(2 * p + core), :] + pair2_recv[p, heads].astype(f32)

    def to_owner2(i):
        def body(j):
            p = lax.rem(chip + 1 + j, half)
            chip2_send[p, pl.ds(i * middle, middle)] = merge2(i, p).astype(bf16)
            chip_copy(2 + i, p, chip).start()

        loop(0, half - 1, body)
        turn[pl.ds(i * middle, middle)] = merge2(i, chip)

    def add2(i):
        heads = pl.ds(i * middle, middle)

        def body(k, acc):
            p = source_of(k)
            chip_copy(2 + i, p, p).wait_recv()
            return acc + chip2_recv[p, heads].astype(f32)

        turn[heads] = lax.fori_loop(1, half, body, turn[heads])

    loop(0, middle, down)
    to_pair2(0)
    loop(middle, middle + 2, down)
    to_owner2(0)
    loop(middle + 2, KEY_VALUE_HEADS, down)
    to_pair2(1)
    to_owner2(1)
    add2(0)
    add2(1)
    out_ref[...] = jnp.concatenate(
        [
            turn[g, pl.ds(h, rows, stride=GROUP), :]
            for g in range(KEY_VALUE_HEADS)
            for h in range(GROUP)
        ],
        axis=1,
    ).astype(bf16)
    finish_sends(2)
    finish_sends(3)


def local(queries, keys, values, position, lengths, gain, gate_weight, up_weight, down_weight):
    n = lax.axis_size("ctx")
    half = n // 2
    rows, width = queries.shape
    slots, kv_width = keys.shape
    hidden = gate_weight.shape[0]
    chunk = rows * GROUP
    own = KEY_VALUE_HEADS * GROUP // n
    every = n * rows
    block = (KEY_VALUE_HEADS, chunk, HEAD_SIZE)
    vm = pltpu.VMEM
    data = lambda: vm((half,) + block, bf16)
    state = lambda: vm((half, 8, HEAD_SIZE), f32)
    heads = lambda: vm((half, own * every, HEAD_SIZE), bf16)
    dma = pltpu.SemaphoreType.DMA
    in_vmem = pl.BlockSpec(memory_space=pltpu.VMEM)
    in_hbm = pl.BlockSpec(memory_space=pl.ANY)
    return pl.pallas_call(
        functools.partial(kernel, n, rows),
        out_shape=jax.ShapeDtypeStruct((rows, width), bf16),
        in_specs=[pl.BlockSpec(memory_space=pltpu.SMEM)] + [in_vmem] * 3 + [in_hbm] * 5,
        out_specs=in_vmem,
        scratch_shapes=[
            vm((slots, kv_width), bf16),
            vm((slots, kv_width), bf16),
            vm((hidden, width), bf16),
            vm((hidden, width), bf16),
            vm((hidden, width), bf16),
            vm((n, KEY_VALUE_HEADS + 1, chunk, HEAD_SIZE), bf16),
            vm((n, every, own * HEAD_SIZE), bf16),
            vm((KEY_VALUE_HEADS, n * chunk, HEAD_SIZE), f32),
            vm((KEY_VALUE_HEADS, n * chunk, HEAD_SIZE), f32),
            vm((every, HEAD_SIZE), f32),
            vm((every, hidden), f32),
            vm((every, hidden), f32),
            vm((every, hidden), bf16),
            vm(block, f32),
            heads(), heads(), state(), state(),
            heads(), heads(), state(), state(),
            data(), data(), data(), data(),
            dma((2,)), dma((3, PIECES)),
            dma((2, half // 2 + 1)), dma((2, half)), dma((2, half // 2)), dma((2, n)),
            dma((4, half)), dma((4, half)), dma((4, half)), dma((4, half)),
        ],
        compiler_params=pltpu.CompilerParams(
            collective_id=0, has_side_effects=True, vmem_limit_bytes=60 * 2**20
        ),
    )(
        lengths, queries, position.reshape(1, slots), gain.reshape(1, width),
        keys, values, gate_weight, up_weight, down_weight,
    )


def solution(mesh):
    split = P(("groups", "ctx"))
    tall = P(("groups", "ctx"), None)
    weight = P("ctx", None)
    return jax.shard_map(
        local,
        mesh=mesh,
        in_specs=(tall, tall, tall, split, split, P(), weight, weight, weight),
        out_specs=tall,
        check_vma=False,
    )
```
